1024 devices in a mesh: row: 16 (over z_lo, x), col: 64 (over y, z_hi, core).
Axes of the slice: x: 4, y: 8, z: 16 (z_hi: 4, z_lo: 4; z = z_hi * 4 + z_lo), core: 2. Of those that a mesh axis runs over, the one named last changes fastest.
Arguments:
- xvals: bfloat16 [2048, 64, 640], P(('row', 'col')), may hold values from -0.3125 to 0.3125
- cols: int32 [2048, 10], replicated, may hold values from 0 to 2047, as said below
- counts: int32 [2048], replicated, may hold values from 1 to 10
Outputs:
- sign_step: float32 [2048, 64, 640], P(('row', 'col'))
The draws below stay inside these ranges and needn't reach their ends.
Inputs may be any that keep to these rules, and one draw needn't show every extreme that they name: cols[i, 0] = i; the 10 block columns of block row i are distinct, and each is a block row held by the device that holds block row i or by one of that device's four neighbours along row or col, the ends of each axis being joined.
All inputs are finite; a program needn't handle non-finite values.
Results may differ from the reference program's by a relative error of at most 0.005.
Values may be sent and summed in bfloat16 or wider, within the bound.
A program may use at most 32 MiB of HBM per device.

```python
import jax
import jax.numpy as jnp
from jax import lax

BLOCK = 64
SLOTS = 10
ROWS_DEV = 2
ITERS = 2
NB = 2048
N_ROW = 16
N_COL = 64


def draw_cols(key, part):
    key = jax.random.fold_in(key, 11)
    row_ids = jnp.arange(NB, dtype=jnp.int32)
    device = row_ids // ROWS_DEV
    grid_row = device // N_COL
    grid_col = device % N_COL
    lower_row = (grid_row + N_ROW - 1) % N_ROW
    upper_row = (grid_row + 1) % N_ROW
    lower_col = (grid_col + N_COL - 1) % N_COL
    upper_col = (grid_col + 1) % N_COL
    devices = jnp.stack([device, lower_row * N_COL + grid_col, upper_row * N_COL + grid_col, grid_row * N_COL + lower_col, grid_row * N_COL + upper_col], axis=1)
    local_rows = jnp.arange(ROWS_DEV, dtype=jnp.int32)
    candidates = (devices[:, :, None] * ROWS_DEV + local_rows[None, None, :]).reshape(NB, 5 * ROWS_DEV)
    scores = jax.random.randint(key, (NB, 5 * ROWS_DEV), 0, 1 << 20)
    positions = jnp.arange(5 * ROWS_DEV, dtype=jnp.int32)
    scores = scores * (5 * ROWS_DEV) + positions[None, :]
    scores = jnp.where(candidates == row_ids[:, None], -1, scores)
    ranking = jnp.argsort(scores, axis=1, stable=True)
    chosen = jnp.take_along_axis(candidates, ranking[:, :SLOTS], axis=1)
    return chosen.astype(jnp.int32)


def draw_counts(key, part):
    key = jax.random.fold_in(key, 23)
    drawn_counts = jax.random.randint(key, (NB,), 1, SLOTS + 1)
    row_ids = jnp.arange(NB, dtype=jnp.int32)
    filled = jnp.where(row_ids % 7 == 3, 1, drawn_counts)
    return jnp.where(row_ids % 5 == 0, SLOTS, filled).astype(jnp.int32)


def shard_levels(own_key, shape, pieces, low, largest):
    factor_of, own = 1.0, jax.random.fold_in(own_key, 6)
    for axis_at, parts in pieces:
        heights = jnp.exp(jax.random.uniform(jax.random.fold_in(own, axis_at), (parts,), jnp.float32, low / len(pieces), largest / len(pieces)))
        factor_of = factor_of * jnp.repeat(heights, shape[axis_at] // parts).reshape([-1 if axis == axis_at else 1 for axis in range(len(shape))])
    return factor_of


def bell_draw(key, extent, deviation, limit, pieces=(), kind=jnp.bfloat16):
    gain = shard_levels(key, extent, pieces, -0.22, 0.18) if pieces else 1.0
    drawn = jax.random.normal(key, extent, jnp.float32) * deviation * gain
    return jnp.minimum(jnp.maximum(drawn, -limit), limit).astype(kind)


def setup_inputs(seed: int = 0) -> dict:
    key_list = jax.random.split(jax.random.key(seed), 4)
    xvals = bell_draw(key_list[0], (NB, BLOCK, SLOTS * BLOCK), (BLOCK * SLOTS // 2) ** -0.5, 0.3125, ((0, 1024),))
    cols = draw_cols(jax.random.fold_in(key_list[3], 71), 0)
    counts = draw_counts(jax.random.fold_in(key_list[3], 71), 0)
    return {"xvals": xvals, "cols": cols, "counts": counts}


def block_index(cols, counts):
    slot_ids = jnp.arange(SLOTS, dtype=jnp.int32)
    live_slot = slot_ids[None, :] < counts[:, None]

    def one_row(row_id):
        own_cols = cols[row_id]
        own_live = live_slot[row_id]
        partner_cols = cols[own_cols]
        partner_live = live_slot[own_cols]
        matches = (partner_cols[:, :, None] == own_cols[None, None, :]) & partner_live[:, :, None]
        present = jnp.any(matches, axis=1)
        matched_slot = jnp.sum(matches.astype(jnp.int32) * slot_ids[None, :, None], axis=1)
        wanted = present & own_live[:, None] & own_live[None, :]
        return jnp.where(wanted, own_cols[:, None] * SLOTS + matched_slot, NB * SLOTS).astype(jnp.int32)

    return lax.map(one_row, jnp.arange(NB, dtype=jnp.int32))


def reference(xvals, cols, counts):
    lookup = block_index(cols, counts)
    slot_ids = jnp.arange(SLOTS, dtype=jnp.int32)
    identity = jnp.eye(BLOCK, dtype=jnp.float32)
    diagonal_part = 3.0 * identity[:, None, :] * (slot_ids == 0).astype(jnp.float32)[None, :, None]
    current = xvals
    result = jnp.zeros((NB, BLOCK, SLOTS * BLOCK), jnp.float32)
    for sweep in range(ITERS):
        stored = current.reshape(NB, BLOCK, SLOTS, BLOCK)
        blocks_flat = jnp.transpose(stored, (0, 2, 1, 3)).reshape(NB * SLOTS, BLOCK, BLOCK)
        blocks_flat = jnp.concatenate([blocks_flat, jnp.zeros((1, BLOCK, BLOCK), blocks_flat.dtype)], axis=0)

        def advance(row_id, stored=stored, blocks_flat=blocks_flat):
            gathered = blocks_flat[lookup[row_id]].astype(jnp.float32)
            left_blocks = stored[row_id].astype(jnp.float32)
            square = jnp.einsum("apb,pqbc->aqc", left_blocks, gathered)
            shifted = (diagonal_part - square).astype(jnp.bfloat16)
            shifted = lax.optimization_barrier(shifted).astype(jnp.float32)
            return 0.5 * jnp.einsum("apb,pqbc->aqc", shifted, gathered)

        result = lax.map(advance, jnp.arange(NB, dtype=jnp.int32)).reshape(NB, BLOCK, SLOTS * BLOCK)
        current = result.astype(jnp.bfloat16)
    return result
```

```python
import functools

import jax
import jax.numpy as jnp
from jax import lax
from jax.experimental import pallas as pl
from jax.experimental.pallas import tpu as pltpu
from jax.sharding import PartitionSpec as P

MESH = pl.DeviceIdType.MESH
F32 = jnp.float32
BF16 = jnp.bfloat16


def dot(a, b):
    return jnp.dot(a, b, preferred_element_type=F32)


def kernel(
    row_count, col_count, block, slots,
    x_hbm, cols_hbm, counts_hbm, out_hbm,
    xs, tiles, cnts, can, toward, diag, s0, s0_in, y0, y0_in, outv,
    local_sem, send_sem, recv_sem,
):
    pair = 2 * block
    r = lax.axis_index("row")
    c = lax.axis_index("col")
    up, down = lax.rem(r + row_count - 1, row_count), lax.rem(r + 1, row_count)
    left, right = lax.rem(c + col_count - 1, col_count), lax.rem(c + 1, col_count)
    places = [(up, c), (down, c), (r, left), (r, right)]

    barrier = pltpu.get_barrier_semaphore()
    for place in places:
        pl.semaphore_signal(barrier, inc=1, device_id=place, device_id_type=MESH)

    width = 2 * col_count
    loads = []
    for at, grid_row in enumerate((r, up, down)):
        lanes = pl.ds(pl.multiple_of(grid_row * width, width), width)
        loads.append(
            pltpu.make_async_copy(cols_hbm.at[:, lanes], tiles.at[at], local_sem.at[at])
        )
    loads.append(pltpu.make_async_copy(counts_hbm, cnts, local_sem.at[3]))
    loads.append(pltpu.make_async_copy(x_hbm, xs, local_sem.at[4]))
    for load in loads:
        load.start()

    lane = lax.broadcasted_iota(jnp.int32, (1, pair), 1)
    second = (lane >= block).astype(jnp.int32)
    tile_lane = lax.broadcasted_iota(jnp.int32, (1, width), 1)
    slot_id = lax.broadcasted_iota(jnp.int32, (slots, 1), 0).astype(F32)
    devices = [r * col_count + c] + [a * col_count + b for a, b in places]
    wide = [(2 * device + second).astype(F32) for device in devices]

    def stored_row(at, grid_row, grid_col, which):
        here = tile_lane == 2 * grid_col + which
        ids = jnp.sum(jnp.where(here, tiles[at].astype(F32), 0.0), axis=1, keepdims=True)
        count_row = cnts[pl.ds(grid_row, 1), :].astype(F32)
        count = jnp.sum(jnp.where(here, count_row, 0.0), axis=1, keepdims=True)
        return jnp.where(slot_id < count, ids, -1.0)

    for load in loads[:4]:
        load.wait()
    own = [stored_row(0, r, c, which) for which in range(2)]
    masks = [[(own[i] == wide[g]) for g in range(5)] for i in range(2)]

    def live(parts):
        return jnp.concatenate(
            [
                jnp.broadcast_to(
                    jnp.max(part.astype(F32), axis=0, keepdims=True), (block, pair)
                )
                for part in parts
            ],
            axis=0,
        )

    first_half = lane < block
    loads[4].wait()
    for i in range(2):
        sums = [jnp.zeros((block, pair), F32) for _ in range(5)]
        for j in range(slots // 2):
            both = xs[i, :, j * pair : (j + 1) * pair].astype(F32)
            turned = pltpu.roll(both, block, 1)
            for slot, doubled in (
                (2 * j, jnp.where(first_half, both, turned)),
                (2 * j + 1, jnp.where(first_half, turned, both)),
            ):
                for g in range(5):
                    sums[g] = jnp.where(masks[i][g][slot : slot + 1], doubled, sums[g])
        for g in range(5):
            can[g, i * block : (i + 1) * block, :] = sums[g].astype(BF16)

    pl.semaphore_wait(barrier, 4)
    order = (2, 3, 0, 1)

    def send(src, dst, kind, e):
        copy = pltpu.make_async_remote_copy(
            src_ref=src,
            dst_ref=dst.at[e ^ 1],
            send_sem=send_sem.at[kind, e],
            recv_sem=recv_sem.at[kind, e ^ 1],
            device_id=places[e],
            device_id_type=MESH,
        )
        copy.start()
        return copy

    def arrival(dst, kind, e):
        return pltpu.make_async_remote_copy(
            src_ref=dst.at[e],
            dst_ref=dst.at[e],
            send_sem=send_sem.at[kind, e],
            recv_sem=recv_sem.at[kind, e],
            device_id=places[e],
            device_id_type=MESH,
        )

    sent = [send(can.at[e + 1], toward, 0, e) for e in order]
    sent += [send(can.at[0], diag, 1, e) for e in order]

    own_live = [live([masks[i][g] for i in range(2)]) for g in range(5)]
    near_live = []
    for e, (at, (grid_row, grid_col)) in enumerate(zip((1, 2, 0, 0), places)):
        rows = [stored_row(at, grid_row, grid_col, which) for which in range(2)]
        near_live.append(live([row == wide[0] for row in rows]))
    x0 = can[0]
    xe = [can[e + 1] for e in range(4)]
    square = dot(x0, x0)
    x0_xe = [dot(x0, xe[e]) for e in range(4)]
    eye = lax.broadcasted_iota(jnp.int32, (pair, pair), 0) == lax.broadcasted_iota(
        jnp.int32, (pair, pair), 1
    )
    three = jnp.where(eye, 3.0, 0.0)

    for e in order:
        arrival(toward, 0, e).wait_recv()
        square += dot(xe[e], toward[e])
    s0[...] = (three - square * own_live[0]).astype(BF16)
    sent += [send(s0, s0_in, 2, e) for e in order]

    near_s = [dot(toward[e], x0) for e in range(4)]
    following = dot(s0[...], x0)
    side_s = [None] * 4
    for e in order:
        arrival(diag, 1, e).wait_recv()
        side = x0_xe[e] + dot(xe[e], diag[e])
        side_s[e] = (-side * own_live[e + 1]).astype(BF16)
        following += dot(side_s[e], toward[e])
    y0[...] = (0.5 * following * own_live[0]).astype(BF16)
    sent += [send(y0, y0_in, 3, e) for e in order]

    ye = []
    near_part = []
    for e in range(4):
        side = dot(s0[...], xe[e]) + dot(side_s[e], diag[e])
        ye.append((0.5 * side * own_live[e + 1]).astype(BF16))
        near = near_s[e] + dot(diag[e], toward[e])
        near = (-near * near_live[e]).astype(BF16)
        near_part.append(dot(near, x0))
    square = dot(y0[...], y0[...])
    y0_ye = [dot(y0[...], ye[e]) for e in range(4)]
    near_y = [None] * 4
    for e in order:
        arrival(s0_in, 2, e).wait_recv()
        near = near_part[e] + dot(s0_in[e], toward[e])
        near_y[e] = (0.5 * near * near_live[e]).astype(BF16)
        square += dot(ye[e], near_y[e])
    last_s = (three - square * own_live[0]).astype(BF16)
    results = [dot(last_s, y0[...])] + [dot(last_s, ye[e]) for e in range(4)]
    for e in order:
        arrival(y0_in, 3, e).wait_recv()
        side = y0_ye[e] + dot(ye[e], y0_in[e])
        side = (-side * own_live[e + 1]).astype(BF16)
        results[0] += dot(side, near_y[e])
        results[e + 1] += dot(side, y0_in[e])

    stores = []
    place_id = lax.broadcasted_iota(jnp.int32, (slots, 1), 0)
    holder = jnp.zeros((slots, 1), jnp.int32)
    for g in range(5):
        holder = jnp.where(place_id // 2 == g, devices[g], holder)
    candidate = (2 * holder + place_id % 2).astype(F32)
    for i in range(2):
        chosen = []
        for j in range(slots // 2):
            names = jnp.where(first_half, own[i][2 * j : 2 * j + 1], own[i][2 * j + 1 : 2 * j + 2])
            chosen.append(candidate == names)
        sums = [jnp.zeros((block, pair), F32) for _ in range(5)]
        for g in range(5):
            both = 0.5 * results[g][i * block : (i + 1) * block, :]
            turned = pltpu.roll(both, block, 1)
            for spot, doubled in (
                (2 * g, jnp.where(first_half, both, turned)),
                (2 * g + 1, jnp.where(first_half, turned, both)),
            ):
                for j in range(slots // 2):
                    sums[j] = jnp.where(chosen[j][spot : spot + 1], doubled, sums[j])
        for j in range(slots // 2):
            outv[i, :, j * pair : (j + 1) * pair] = sums[j]
        store = pltpu.make_async_copy(outv.at[i], out_hbm.at[i], local_sem.at[5 + i])
        store.start()
        stores.append(store)
    for copy in sent:
        copy.wait_send()
    for store in stores:
        store.wait()


def per_device(xvals, cols, counts):
    rows_here, block, _ = xvals.shape
    slots = cols.shape[1]
    row_count = lax.axis_size("row")
    col_count = lax.axis_size("col")
    width = rows_here * col_count
    pair = 2 * block
    square = (pair, pair)
    any_space = pl.BlockSpec(memory_space=pl.ANY)
    return pl.pallas_call(
        functools.partial(kernel, row_count, col_count, block, slots),
        out_shape=jax.ShapeDtypeStruct(xvals.shape, F32),
        in_specs=[any_space] * 3,
        out_specs=any_space,
        scratch_shapes=[
            pltpu.VMEM(xvals.shape, BF16),
            pltpu.VMEM((3, slots, width), jnp.int32),
            pltpu.VMEM((row_count, width), jnp.int32),
            pltpu.VMEM((5,) + square, BF16),
            pltpu.VMEM((4,) + square, BF16),
            pltpu.VMEM((4,) + square, BF16),
            pltpu.VMEM(square, BF16),
            pltpu.VMEM((4,) + square, BF16),
            pltpu.VMEM(square, BF16),
            pltpu.VMEM((4,) + square, BF16),
            pltpu.VMEM(xvals.shape, F32),
            pltpu.SemaphoreType.DMA((7,)),
            pltpu.SemaphoreType.DMA((4, 4)),
            pltpu.SemaphoreType.DMA((4, 4)),
        ],
        compiler_params=pltpu.CompilerParams(
            collective_id=0, has_side_effects=True, vmem_limit_bytes=60 * 1024 * 1024
        ),
        cost_estimate=pl.CostEstimate(
            flops=250_000_000, bytes_accessed=600_000, transcendentals=0
        ),
        name="sign_steps",
    )(xvals, cols.T, counts.reshape(row_count, width))


def solution(mesh):
    return jax.shard_map(
        per_device,
        mesh=mesh,
        in_specs=(P(("row", "col"), None, None), P(), P()),
        out_specs=P(("row", "col"), None, None),
        check_vma=False,
    )
```

```python
import functools

import jax
import jax.numpy as jnp
from jax import lax
from jax.experimental import pallas as pl
from jax.experimental.pallas import tpu as pltpu
from jax.sharding import PartitionSpec as P

MESH = pl.DeviceIdType.MESH
F32 = jnp.float32
BF16 = jnp.bfloat16


def dot(a, b):
    return jnp.dot(a, b, preferred_element_type=F32)


def kernel(
    row_count, col_count, block, slots,
    x_hbm, cols_hbm, counts_hbm, out_hbm,
    xs, tiles, cnts, can, toward, diag, s0, s0_in, y0, y0_in, part_a, part_b, outv,
    local_sem, send_sem, recv_sem, hello,
):
    pair = 2 * block
    r = lax.axis_index("row")
    c = lax.axis_index("col")
    up, down = lax.rem(r + row_count - 1, row_count), lax.rem(r + 1, row_count)
    odd = lax.rem(c, 2)
    beside = c + 1 - 2 * odd
    beyond = lax.rem(c + col_count - 1 + 2 * odd, col_count)
    places = [(up, c), (down, c), (r, beside), (r, beyond)]
    back = (1, 0, 2, 3)
    near, far = (0, 1, 2), 3

    def rank(row, col):
        z = lax.rem(lax.div(col, 2), 4) * 4 + lax.div(row, 4)
        usual = (z * 64 + lax.div(col, 8)) * 8 + lax.rem(row, 4) * 2 + lax.rem(col, 2)
        return jnp.where(row + col == 0, 12 * 512 - 1, usual)

    mine = rank(r, c)
    later = [rank(*place) > mine for place in places]
    barrier = pltpu.get_barrier_semaphore()
    for e in range(4):

        @pl.when(later[e])
        def _(e=e):
            pl.semaphore_signal(barrier, inc=1, device_id=places[e], device_id_type=MESH)

    width = 2 * col_count
    loads = []
    for at, grid_row in enumerate((r, up, down)):
        lanes = pl.ds(pl.multiple_of(grid_row * width, width), width)
        loads.append(
            pltpu.make_async_copy(cols_hbm.at[:, lanes], tiles.at[at], local_sem.at[at])
        )
    loads.append(pltpu.make_async_copy(counts_hbm, cnts, local_sem.at[3]))
    loads.append(pltpu.make_async_copy(x_hbm, xs, local_sem.at[4]))
    for load in loads:
        load.start()

    earlier = sum(1 - late.astype(jnp.int32) for late in later)

    @pl.when(earlier > 0)
    def _():
        pl.semaphore_wait(barrier, earlier)

    for e in range(4):

        @pl.when(jnp.logical_not(later[e]))
        def _(e=e):
            pl.semaphore_signal(
                hello.at[back[e]], inc=1, device_id=places[e], device_id_type=MESH
            )

    lane = lax.broadcasted_iota(jnp.int32, (1, pair), 1)
    second = (lane >= block).astype(jnp.int32)
    tile_lane = lax.broadcasted_iota(jnp.int32, (1, width), 1)
    slot_id = lax.broadcasted_iota(jnp.int32, (slots, 1), 0).astype(F32)
    devices = [r * col_count + c] + [a * col_count + b for a, b in places]
    wide = [(2 * device + second).astype(F32) for device in devices]

    def stored_row(at, grid_row, grid_col, which):
        here = tile_lane == 2 * grid_col + which
        ids = jnp.sum(jnp.where(here, tiles[at].astype(F32), 0.0), axis=1, keepdims=True)
        count_row = cnts[pl.ds(grid_row, 1), :].astype(F32)
        count = jnp.sum(jnp.where(here, count_row, 0.0), axis=1, keepdims=True)
        return jnp.where(slot_id < count, ids, -1.0)

    for load in loads[:4]:
        load.wait()
    own = [stored_row(0, r, c, which) for which in range(2)]
    masks = [[(own[i] == wide[g]) for g in range(5)] for i in range(2)]

    def live(parts):
        return jnp.concatenate(
            [
                jnp.broadcast_to(
                    jnp.max(part.astype(F32), axis=0, keepdims=True), (block, pair)
                )
                for part in parts
            ],
            axis=0,
        )

    first_half = lane < block
    loads[4].wait()
    for i in range(2):
        sums = [jnp.zeros((block, pair), F32) for _ in range(5)]
        for j in range(slots // 2):
            both = xs[i, :, j * pair : (j + 1) * pair].astype(F32)
            turned = pltpu.roll(both, block, 1)
            for slot, doubled in (
                (2 * j, jnp.where(first_half, both, turned)),
                (2 * j + 1, jnp.where(first_half, turned, both)),
            ):
                for g in range(5):
                    sums[g] = jnp.where(masks[i][g][slot : slot + 1], doubled, sums[g])
        for g in range(5):
            can[g, i * block : (i + 1) * block, :] = sums[g].astype(BF16)

    sent = []

    def post(src, dst, kind, e):
        copy = pltpu.make_async_remote_copy(
            src_ref=src,
            dst_ref=dst.at[back[e]],
            send_sem=send_sem.at[kind, e],
            recv_sem=recv_sem.at[kind, back[e]],
            device_id=places[e],
            device_id_type=MESH,
        )
        sent.append(copy)
        return copy

    def arrival(dst, kind, e):
        return pltpu.make_async_remote_copy(
            src_ref=dst.at[e],
            dst_ref=dst.at[e],
            send_sem=send_sem.at[kind, e],
            recv_sem=recv_sem.at[kind, e],
            device_id=places[e],
            device_id_type=MESH,
        )

    first = [
        [post(can.at[e + 1], toward, 0, e), post(can.at[0], diag, 1, e)] for e in range(4)
    ]
    sums_a = post(part_a, s0_in, 2, far)
    sums_b = post(part_b, y0_in, 3, far)

    @pl.when(jnp.logical_not(later[far]))
    def _():
        for copy in first[far]:
            copy.start()

    for e in near:

        @pl.when(later[e])
        def _(e=e):
            pl.semaphore_wait(hello.at[e], 1)

        for copy in first[e]:
            copy.start()

    own_live = [live([masks[i][g] for i in range(2)]) for g in range(5)]
    near_live = []
    for e, (at, (grid_row, grid_col)) in enumerate(zip((1, 2, 0, 0), places)):
        rows = [stored_row(at, grid_row, grid_col, which) for which in range(2)]
        near_live.append(live([row == wide[0] for row in rows]))
        if e == far:
            far_live = live([row == wide[far + 1] for row in rows])
    x0 = can[0]
    xe = [can[e + 1] for e in range(4)]
    square = dot(x0, x0)
    x0_xe = [dot(x0, xe[e]) for e in range(4)]
    eye = lax.broadcasted_iota(jnp.int32, (pair, pair), 0) == lax.broadcasted_iota(
        jnp.int32, (pair, pair), 1
    )
    three = jnp.where(eye, 3.0, 0.0)

    for e in near:
        arrival(toward, 0, e).wait_recv()
        square += dot(xe[e], toward[e])
    part_a[...] = square.astype(BF16)

    @pl.when(jnp.logical_not(later[far]))
    def _():
        sums_a.start()

    side_s = [None] * 4
    following = jnp.zeros((pair, pair), F32)
    for e in near:
        arrival(diag, 1, e).wait_recv()
        side = x0_xe[e] + dot(xe[e], diag[e])
        side_s[e] = (-side * own_live[e + 1]).astype(BF16)
        following += dot(side_s[e], toward[e])
    part_b[...] = following.astype(BF16)

    @pl.when(jnp.logical_not(later[far]))
    def _():
        sums_b.start()

    @pl.when(later[far])
    def _():
        pl.semaphore_wait(hello.at[far], 1)
        for copy in first[far] + [sums_a, sums_b]:
            copy.start()


    arrival(toward, 0, far).wait_recv()
    square += dot(xe[far], toward[far])
    s0[...] = (three - square * own_live[0]).astype(BF16)
    for e in near:
        post(s0, s0_in, 2, e).start()
    added = dot(s0[...], x0)
    arrival(diag, 1, far).wait_recv()
    side = x0_xe[far] + dot(xe[far], diag[far])
    side_s[far] = (-side * own_live[far + 1]).astype(BF16)
    added += dot(side_s[far], toward[far])
    y0[...] = (0.5 * (following + added) * own_live[0]).astype(BF16)
    for e in near:
        post(y0, y0_in, 3, e).start()

    ye = []
    near_part = []
    for e in range(4):
        side = dot(s0[...], xe[e]) + dot(side_s[e], diag[e])
        ye.append((0.5 * side * own_live[e + 1]).astype(BF16))
        theirs = dot(toward[e], x0) + dot(diag[e], toward[e])
        theirs = (-theirs * near_live[e]).astype(BF16)
        near_part.append(dot(theirs, x0))
    far_square = dot(toward[far], xe[far])
    far_following = dot(theirs, xe[far])
    square = dot(y0[...], y0[...])
    y0_ye = [dot(y0[...], ye[e]) for e in range(4)]
    near_y = [None] * 4
    for e in near:
        arrival(s0_in, 2, e).wait_recv()
        theirs = near_part[e] + dot(s0_in[e], toward[e])
        near_y[e] = (0.5 * theirs * near_live[e]).astype(BF16)
        square += dot(ye[e], near_y[e])
    arrival(s0_in, 2, far).wait_recv()
    far_s0 = (three - (far_square + s0_in[far].astype(F32)) * far_live).astype(BF16)
    theirs = near_part[far] + dot(far_s0, toward[far])
    near_y[far] = (0.5 * theirs * near_live[far]).astype(BF16)
    square += dot(ye[far], near_y[far])
    last_s = (three - square * own_live[0]).astype(BF16)
    far_following += dot(far_s0, diag[far])
    results = [dot(last_s, y0[...])] + [dot(last_s, ye[e]) for e in range(4)]
    for e in range(4):
        arrival(y0_in, 3, e).wait_recv()
        theirs = y0_in[e]
        if e == far:
            theirs = (0.5 * (far_following + theirs.astype(F32)) * far_live).astype(BF16)
        side = y0_ye[e] + dot(ye[e], theirs)
        side = (-side * own_live[e + 1]).astype(BF16)
        results[0] += dot(side, near_y[e])
        results[e + 1] += dot(side, theirs)

    stores = []
    place_id = lax.broadcasted_iota(jnp.int32, (slots, 1), 0)
    holder = jnp.zeros((slots, 1), jnp.int32)
    for g in range(5):
        holder = jnp.where(place_id // 2 == g, devices[g], holder)
    candidate = (2 * holder + place_id % 2).astype(F32)
    for i in range(2):
        chosen = []
        for j in range(slots // 2):
            names = jnp.where(first_half, own[i][2 * j : 2 * j + 1], own[i][2 * j + 1 : 2 * j + 2])
            chosen.append(candidate == names)
        sums = [jnp.zeros((block, pair), F32) for _ in range(5)]
        for g in range(5):
            both = 0.5 * results[g][i * block : (i + 1) * block, :]
            turned = pltpu.roll(both, block, 1)
            for spot, doubled in (
                (2 * g, jnp.where(first_half, both, turned)),
                (2 * g + 1, jnp.where(first_half, turned, both)),
            ):
                for j in range(slots // 2):
                    sums[j] = jnp.where(chosen[j][spot : spot + 1], doubled, sums[j])
        for j in range(slots // 2):
            outv[i, :, j * pair : (j + 1) * pair] = sums[j]
        store = pltpu.make_async_copy(outv.at[i], out_hbm.at[i], local_sem.at[5 + i])
        store.start()
        stores.append(store)
    for copy in sent:
        copy.wait_send()
    for store in stores:
        store.wait()


def per_device(xvals, cols, counts):
    rows_here, block, _ = xvals.shape
    slots = cols.shape[1]
    row_count = lax.axis_size("row")
    col_count = lax.axis_size("col")
    width = rows_here * col_count
    pair = 2 * block
    square = (pair, pair)
    any_space = pl.BlockSpec(memory_space=pl.ANY)
    return pl.pallas_call(
        functools.partial(kernel, row_count, col_count, block, slots),
        out_shape=jax.ShapeDtypeStruct(xvals.shape, F32),
        in_specs=[any_space] * 3,
        out_specs=any_space,
        scratch_shapes=[
            pltpu.VMEM(xvals.shape, BF16),
            pltpu.VMEM((3, slots, width), jnp.int32),
            pltpu.VMEM((row_count, width), jnp.int32),
            pltpu.VMEM((5,) + square, BF16),
            pltpu.VMEM((4,) + square, BF16),
            pltpu.VMEM((4,) + square, BF16),
            pltpu.VMEM(square, BF16),
            pltpu.VMEM((4,) + square, BF16),
            pltpu.VMEM(square, BF16),
            pltpu.VMEM((4,) + square, BF16),
            pltpu.VMEM(square, BF16),
            pltpu.VMEM(square, BF16),
            pltpu.VMEM(xvals.shape, F32),
            pltpu.SemaphoreType.DMA((7,)),
            pltpu.SemaphoreType.DMA((4, 4)),
            pltpu.SemaphoreType.DMA((4, 4)),
            pltpu.SemaphoreType.REGULAR((4,)),
        ],
        compiler_params=pltpu.CompilerParams(
            collective_id=0, has_side_effects=True, vmem_limit_bytes=60 * 1024 * 1024
        ),
        cost_estimate=pl.CostEstimate(
            flops=250_000_000, bytes_accessed=600_000, transcendentals=0
        ),
        name="sign_steps",
    )(xvals, cols.T, counts.reshape(row_count, width))


def solution(mesh):
    return jax.shard_map(
        per_device,
        mesh=mesh,
        in_specs=(P(("row", "col"), None, None), P(), P()),
        out_specs=P(("row", "col"), None, None),
        check_vma=False,
    )
```

```python
import functools

import jax
import jax.numpy as jnp
from jax import lax
from jax.experimental import pallas as pl
from jax.experimental.pallas import tpu as pltpu
from jax.sharding import PartitionSpec as P

MESH = pl.DeviceIdType.MESH
F32 = jnp.float32
BF16 = jnp.bfloat16


def dot(a, b):
    return jnp.dot(a, b, preferred_element_type=F32)


def kernel(
    row_count, col_count, block, slots,
    x_hbm, cols_hbm, counts_hbm, out_hbm,
    xs, tiles, cnts, can, toward, diag, s0, s0_in, y0, y0_in, part_a, part_b, outv,
    local_sem, send_sem, recv_sem, hello,
):
    pair = 2 * block
    r = lax.axis_index("row")
    c = lax.axis_index("col")
    up, down = lax.rem(r + row_count - 1, row_count), lax.rem(r + 1, row_count)
    odd = lax.rem(c, 2)
    beside = c + 1 - 2 * odd
    beyond = lax.rem(c + col_count - 1 + 2 * odd, col_count)
    places = [(up, c), (down, c), (r, beside), (r, beyond)]
    back = (1, 0, 2, 3)
    near, far = (0, 1, 2), 3

    width = 2 * col_count
    loads = []
    for at, grid_row in enumerate((r, up, down)):
        lanes = pl.ds(pl.multiple_of(grid_row * width, width), width)
        loads.append(
            pltpu.make_async_copy(cols_hbm.at[:, lanes], tiles.at[at], local_sem.at[at])
        )
    loads.append(pltpu.make_async_copy(counts_hbm, cnts, local_sem.at[3]))
    loads.append(pltpu.make_async_copy(x_hbm, xs, local_sem.at[4]))
    for load in loads[::-1]:
        load.start()

    def rank(row, col):
        z = lax.rem(lax.div(col, 2), 4) * 4 + lax.div(row, 4)
        usual = (z * 64 + lax.div(col, 8)) * 8 + lax.rem(row, 4) * 2 + lax.rem(col, 2)
        return jnp.where(row + col == 0, 12 * 512 - 1, usual)

    mine = rank(r, c)
    later = [rank(*place) > mine for place in places]
    barrier = pltpu.get_barrier_semaphore()
    for e in range(4):

        @pl.when(later[e])
        def _(e=e):
            pl.semaphore_signal(barrier, inc=1, device_id=places[e], device_id_type=MESH)

    lane = lax.broadcasted_iota(jnp.int32, (1, pair), 1)
    second = (lane >= block).astype(jnp.int32)
    tile_lane = lax.broadcasted_iota(jnp.int32, (1, width), 1)
    slot_id = lax.broadcasted_iota(jnp.int32, (slots, 1), 0).astype(F32)
    devices = [r * col_count + c] + [a * col_count + b for a, b in places]
    wide = [(2 * device + second).astype(F32) for device in devices]

    def stored_row(at, grid_row, grid_col, which):
        here = tile_lane == 2 * grid_col + which
        ids = jnp.sum(jnp.where(here, tiles[at].astype(F32), 0.0), axis=1, keepdims=True)
        count_row = cnts[pl.ds(grid_row, 1), :].astype(F32)
        count = jnp.sum(jnp.where(here, count_row, 0.0), axis=1, keepdims=True)
        return jnp.where(slot_id < count, ids, -1.0)

    for load in loads[:4]:
        load.wait()
    own = [stored_row(0, r, c, which) for which in range(2)]
    masks = [[(own[i] == wide[g]) for g in range(5)] for i in range(2)]

    earlier = sum(1 - late.astype(jnp.int32) for late in later)

    @pl.when(earlier > 0)
    def _():
        pl.semaphore_wait(barrier, earlier)

    for e in range(4):

        @pl.when(jnp.logical_not(later[e]))
        def _(e=e):
            pl.semaphore_signal(
                hello.at[back[e]], inc=1, device_id=places[e], device_id_type=MESH
            )

    def live(parts):
        return jnp.concatenate(
            [
                jnp.broadcast_to(
                    jnp.max(part.astype(F32), axis=0, keepdims=True), (block, pair)
                )
                for part in parts
            ],
            axis=0,
        )

    first_half = lane < block
    loads[4].wait()
    for i in range(2):
        sums = [jnp.zeros((block, pair), F32) for _ in range(5)]
        for j in range(slots // 2):
            both = xs[i, :, j * pair : (j + 1) * pair].astype(F32)
            turned = pltpu.roll(both, block, 1)
            for slot, doubled in (
                (2 * j, jnp.where(first_half, both, turned)),
                (2 * j + 1, jnp.where(first_half, turned, both)),
            ):
                for g in range(5):
                    sums[g] = jnp.where(masks[i][g][slot : slot + 1], doubled, sums[g])
        for g in range(5):
            can[g, i * block : (i + 1) * block, :] = sums[g].astype(BF16)

    sent = []

    def post(src, dst, kind, e):
        copy = pltpu.make_async_remote_copy(
            src_ref=src,
            dst_ref=dst.at[back[e]],
            send_sem=send_sem.at[kind, e],
            recv_sem=recv_sem.at[kind, back[e]],
            device_id=places[e],
            device_id_type=MESH,
        )
        sent.append(copy)
        return copy

    def arrival(dst, kind, e):
        return pltpu.make_async_remote_copy(
            src_ref=dst.at[e],
            dst_ref=dst.at[e],
            send_sem=send_sem.at[kind, e],
            recv_sem=recv_sem.at[kind, e],
            device_id=places[e],
            device_id_type=MESH,
        )

    first = [
        [post(can.at[e + 1], toward, 0, e), post(can.at[0], diag, 1, e)] for e in range(4)
    ]
    sums_a = post(part_a, s0_in, 2, far)
    sums_b = post(part_b, y0_in, 3, far)

    @pl.when(jnp.logical_not(later[far]))
    def _():
        for copy in first[far]:
            copy.start()

    for e in near:

        @pl.when(jnp.logical_not(later[e]))
        def _(e=e):
            for copy in first[e]:
                copy.start()

    for e in near[::-1]:

        @pl.when(later[e])
        def _(e=e):
            pl.semaphore_wait(hello.at[e], 1)
            for copy in first[e]:
                copy.start()

    own_live = [live([masks[i][g] for i in range(2)]) for g in range(5)]
    near_live = []
    for e, (at, (grid_row, grid_col)) in enumerate(zip((1, 2, 0, 0), places)):
        rows = [stored_row(at, grid_row, grid_col, which) for which in range(2)]
        near_live.append(live([row == wide[0] for row in rows]))
        if e == far:
            far_live = live([row == wide[far + 1] for row in rows])
    x0 = can[0]
    xe = [can[e + 1] for e in range(4)]
    square = dot(x0, x0)
    x0_xe = [dot(x0, xe[e]) for e in range(4)]
    eye = lax.broadcasted_iota(jnp.int32, (pair, pair), 0) == lax.broadcasted_iota(
        jnp.int32, (pair, pair), 1
    )
    three = jnp.where(eye, 3.0, 0.0)

    for e in near:
        arrival(toward, 0, e).wait_recv()
        square += dot(xe[e], toward[e])
    part_a[...] = square.astype(BF16)

    @pl.when(jnp.logical_not(later[far]))
    def _():
        sums_a.start()

    side_s = [None] * 4
    following = jnp.zeros((pair, pair), F32)
    for e in near:
        arrival(diag, 1, e).wait_recv()
        side = x0_xe[e] + dot(xe[e], diag[e])
        side_s[e] = (-side * own_live[e + 1]).astype(BF16)
        following += dot(side_s[e], toward[e])
    part_b[...] = following.astype(BF16)

    @pl.when(jnp.logical_not(later[far]))
    def _():
        sums_b.start()

    @pl.when(later[far])
    def _():
        pl.semaphore_wait(hello.at[far], 1)
        for copy in first[far] + [sums_a, sums_b]:
            copy.start()


    arrival(toward, 0, far).wait_recv()
    square += dot(xe[far], toward[far])
    s0[...] = (three - square * own_live[0]).astype(BF16)
    for e in near:
        post(s0, s0_in, 2, e).start()
    added = dot(s0[...], x0)
    arrival(diag, 1, far).wait_recv()
    side = x0_xe[far] + dot(xe[far], diag[far])
    side_s[far] = (-side * own_live[far + 1]).astype(BF16)
    added += dot(side_s[far], toward[far])
    y0[...] = (0.5 * (following + added) * own_live[0]).astype(BF16)
    for e in near:
        post(y0, y0_in, 3, e).start()

    ye = []
    near_part = []
    for e in range(4):
        side = dot(s0[...], xe[e]) + dot(side_s[e], diag[e])
        ye.append((0.5 * side * own_live[e + 1]).astype(BF16))
        theirs = dot(toward[e], x0) + dot(diag[e], toward[e])
        theirs = (-theirs * near_live[e]).astype(BF16)
        near_part.append(dot(theirs, x0))
    far_square = dot(toward[far], xe[far])
    far_following = dot(theirs, xe[far])
    square = dot(y0[...], y0[...])
    y0_ye = [dot(y0[...], ye[e]) for e in range(4)]
    near_y = [None] * 4
    for e in near:
        arrival(s0_in, 2, e).wait_recv()
        theirs = near_part[e] + dot(s0_in[e], toward[e])
        near_y[e] = (0.5 * theirs * near_live[e]).astype(BF16)
        square += dot(ye[e], near_y[e])
    arrival(s0_in, 2, far).wait_recv()
    far_s0 = (three - (far_square + s0_in[far].astype(F32)) * far_live).astype(BF16)
    theirs = near_part[far] + dot(far_s0, toward[far])
    near_y[far] = (0.5 * theirs * near_live[far]).astype(BF16)
    square += dot(ye[far], near_y[far])
    last_s = (three - square * own_live[0]).astype(BF16)
    far_following += dot(far_s0, diag[far])
    results = [dot(last_s, y0[...])] + [dot(last_s, ye[e]) for e in range(4)]
    for e in range(4):
        arrival(y0_in, 3, e).wait_recv()
        theirs = y0_in[e]
        if e == far:
            theirs = (0.5 * (far_following + theirs.astype(F32)) * far_live).astype(BF16)
        side = y0_ye[e] + dot(ye[e], theirs)
        side = (-side * own_live[e + 1]).astype(BF16)
        results[0] += dot(side, near_y[e])
        results[e + 1] += dot(side, theirs)

    stores = []
    place_id = lax.broadcasted_iota(jnp.int32, (slots, 1), 0)
    holder = jnp.zeros((slots, 1), jnp.int32)
    for g in range(5):
        holder = jnp.where(place_id // 2 == g, devices[g], holder)
    candidate = (2 * holder + place_id % 2).astype(F32)
    for i in range(2):
        chosen = []
        for j in range(slots // 2):
            names = jnp.where(first_half, own[i][2 * j : 2 * j + 1], own[i][2 * j + 1 : 2 * j + 2])
            chosen.append(candidate == names)
        sums = [jnp.zeros((block, pair), F32) for _ in range(5)]
        for g in range(5):
            both = 0.5 * results[g][i * block : (i + 1) * block, :]
            turned = pltpu.roll(both, block, 1)
            for spot, doubled in (
                (2 * g, jnp.where(first_half, both, turned)),
                (2 * g + 1, jnp.where(first_half, turned, both)),
            ):
                for j in range(slots // 2):
                    sums[j] = jnp.where(chosen[j][spot : spot + 1], doubled, sums[j])
        for j in range(slots // 2):
            outv[i, :, j * pair : (j + 1) * pair] = sums[j]
        store = pltpu.make_async_copy(outv.at[i], out_hbm.at[i], local_sem.at[5 + i])
        store.start()
        stores.append(store)
    for copy in sent:
        copy.wait_send()
    for store in stores:
        store.wait()


def per_device(xvals, cols, counts):
    rows_here, block, _ = xvals.shape
    slots = cols.shape[1]
    row_count = lax.axis_size("row")
    col_count = lax.axis_size("col")
    width = rows_here * col_count
    pair = 2 * block
    square = (pair, pair)
    any_space = pl.BlockSpec(memory_space=pl.ANY)
    return pl.pallas_call(
        functools.partial(kernel, row_count, col_count, block, slots),
        out_shape=jax.ShapeDtypeStruct(xvals.shape, F32),
        in_specs=[any_space] * 3,
        out_specs=any_space,
        scratch_shapes=[
            pltpu.VMEM(xvals.shape, BF16),
            pltpu.VMEM((3, slots, width), jnp.int32),
            pltpu.VMEM((row_count, width), jnp.int32),
            pltpu.VMEM((5,) + square, BF16),
            pltpu.VMEM((4,) + square, BF16),
            pltpu.VMEM((4,) + square, BF16),
            pltpu.VMEM(square, BF16),
            pltpu.VMEM((4,) + square, BF16),
            pltpu.VMEM(square, BF16),
            pltpu.VMEM((4,) + square, BF16),
            pltpu.VMEM(square, BF16),
            pltpu.VMEM(square, BF16),
            pltpu.VMEM(xvals.shape, F32),
            pltpu.SemaphoreType.DMA((7,)),
            pltpu.SemaphoreType.DMA((4, 4)),
            pltpu.SemaphoreType.DMA((4, 4)),
            pltpu.SemaphoreType.REGULAR((4,)),
        ],
        compiler_params=pltpu.CompilerParams(
            collective_id=0, has_side_effects=True, vmem_limit_bytes=60 * 1024 * 1024
        ),
        cost_estimate=pl.CostEstimate(
            flops=250_000_000, bytes_accessed=600_000, transcendentals=0
        ),
        name="sign_steps",
    )(xvals, cols.T, counts.reshape(row_count, width))


def solution(mesh):
    return jax.shard_map(
        per_device,
        mesh=mesh,
        in_specs=(P(("row", "col"), None, None), P(), P()),
        out_specs=P(("row", "col"), None, None),
        check_vma=False,
    )
```

```python
import functools

import jax
import jax.numpy as jnp
from jax import lax
from jax.experimental import pallas as pl
from jax.experimental.pallas import tpu as pltpu
from jax.sharding import PartitionSpec as P

MESH = pl.DeviceIdType.MESH
F32 = jnp.float32
BF16 = jnp.bfloat16


def dot(a, b):
    return jnp.dot(a, b, preferred_element_type=F32)


def kernel(
    row_count, col_count, block, slots,
    xs, all_cols, cnts, _, out,
    can, toward, diag, s0, s0_in, y0, y0_in, part_a, part_b,
    send_sem, recv_sem, hello,
):
    pair = 2 * block
    r = lax.axis_index("row")
    c = lax.axis_index("col")
    up, down = lax.rem(r + row_count - 1, row_count), lax.rem(r + 1, row_count)
    odd = lax.rem(c, 2)
    beside = c + 1 - 2 * odd
    beyond = lax.rem(c + col_count - 1 + 2 * odd, col_count)
    places = [(up, c), (down, c), (r, beside), (r, beyond)]
    back = (1, 0, 2, 3)
    near, far = (0, 1, 2), 3

    width = 2 * col_count
    tiles = [
        all_cols[:, pl.ds(pl.multiple_of(grid_row * width, width), width)]
        for grid_row in (r, up, down)
    ]

    def rank(row, col):
        z = lax.rem(lax.div(col, 2), 4) * 4 + lax.div(row, 4)
        usual = (z * 64 + lax.div(col, 8)) * 8 + lax.rem(row, 4) * 2 + lax.rem(col, 2)
        return jnp.where(row + col == 0, 12 * 512 - 1, usual)

    mine = rank(r, c)
    later = [rank(*place) > mine for place in places]
    barrier = pltpu.get_barrier_semaphore()
    for e in range(4):

        @pl.when(later[e])
        def _(e=e):
            pl.semaphore_signal(barrier, inc=1, device_id=places[e], device_id_type=MESH)

    lane = lax.broadcasted_iota(jnp.int32, (1, pair), 1)
    second = (lane >= block).astype(jnp.int32)
    tile_lane = lax.broadcasted_iota(jnp.int32, (1, width), 1)
    slot_id = lax.broadcasted_iota(jnp.int32, (slots, 1), 0).astype(F32)
    devices = [r * col_count + c] + [a * col_count + b for a, b in places]
    wide = [(2 * device + second).astype(F32) for device in devices]

    def stored_row(at, grid_row, grid_col, which):
        here = tile_lane == 2 * grid_col + which
        ids = jnp.sum(jnp.where(here, tiles[at].astype(F32), 0.0), axis=1, keepdims=True)
        count_row = cnts[pl.ds(grid_row, 1), :].astype(F32)
        count = jnp.sum(jnp.where(here, count_row, 0.0), axis=1, keepdims=True)
        return jnp.where(slot_id < count, ids, -1.0)

    own = [stored_row(0, r, c, which) for which in range(2)]
    masks = [[(own[i] == wide[g]) for g in range(5)] for i in range(2)]

    earlier = sum(1 - late.astype(jnp.int32) for late in later)

    @pl.when(earlier > 0)
    def _():
        pl.semaphore_wait(barrier, earlier)

    for e in range(4):

        @pl.when(jnp.logical_not(later[e]))
        def _(e=e):
            pl.semaphore_signal(
                hello.at[back[e]], inc=1, device_id=places[e], device_id_type=MESH
            )

    def live(parts):
        return jnp.concatenate(
            [
                jnp.broadcast_to(
                    jnp.max(part.astype(F32), axis=0, keepdims=True), (block, pair)
                )
                for part in parts
            ],
            axis=0,
        )

    first_half = lane < block
    for i in range(2):
        sums = [jnp.zeros((block, pair), F32) for _ in range(5)]
        for j in range(slots // 2):
            both = xs[i, :, j * pair : (j + 1) * pair].astype(F32)
            turned = pltpu.roll(both, block, 1)
            for slot, doubled in (
                (2 * j, jnp.where(first_half, both, turned)),
                (2 * j + 1, jnp.where(first_half, turned, both)),
            ):
                for g in range(5):
                    sums[g] = jnp.where(masks[i][g][slot : slot + 1], doubled, sums[g])
        for g in range(5):
            can[g, i * block : (i + 1) * block, :] = sums[g].astype(BF16)

    sent = []

    def post(src, dst, kind, e):
        copy = pltpu.make_async_remote_copy(
            src_ref=src,
            dst_ref=dst.at[back[e]],
            send_sem=send_sem.at[kind, e],
            recv_sem=recv_sem.at[kind, back[e]],
            device_id=places[e],
            device_id_type=MESH,
        )
        sent.append(copy)
        return copy

    def arrival(dst, kind, e):
        return pltpu.make_async_remote_copy(
            src_ref=dst.at[e],
            dst_ref=dst.at[e],
            send_sem=send_sem.at[kind, e],
            recv_sem=recv_sem.at[kind, e],
            device_id=places[e],
            device_id_type=MESH,
        )

    first = [
        [post(can.at[e + 1], toward, 0, e), post(can.at[0], diag, 1, e)] for e in range(4)
    ]
    sums_a = post(part_a, s0_in, 2, far)
    sums_b = post(part_b, y0_in, 3, far)

    @pl.when(jnp.logical_not(later[far]))
    def _():
        for copy in first[far]:
            copy.start()

    for e in near:

        @pl.when(jnp.logical_not(later[e]))
        def _(e=e):
            for copy in first[e]:
                copy.start()

    for e in near[::-1]:

        @pl.when(later[e])
        def _(e=e):
            pl.semaphore_wait(hello.at[e], 1)
            for copy in first[e]:
                copy.start()

    own_live = [live([masks[i][g] for i in range(2)]) for g in range(5)]
    near_live = []
    for e, (at, (grid_row, grid_col)) in enumerate(zip((1, 2, 0, 0), places)):
        rows = [stored_row(at, grid_row, grid_col, which) for which in range(2)]
        near_live.append(live([row == wide[0] for row in rows]))
        if e == far:
            far_live = live([row == wide[far + 1] for row in rows])
    x0 = can[0]
    xe = [can[e + 1] for e in range(4)]
    square = dot(x0, x0)
    x0_xe = [dot(x0, xe[e]) for e in range(4)]
    eye = lax.broadcasted_iota(jnp.int32, (pair, pair), 0) == lax.broadcasted_iota(
        jnp.int32, (pair, pair), 1
    )
    three = jnp.where(eye, 3.0, 0.0)

    for e in near:
        arrival(toward, 0, e).wait_recv()
        square += dot(xe[e], toward[e])
    part_a[...] = square.astype(BF16)

    @pl.when(jnp.logical_not(later[far]))
    def _():
        sums_a.start()

    side_s = [None] * 4
    following = jnp.zeros((pair, pair), F32)
    for e in near:
        arrival(diag, 1, e).wait_recv()
        side = x0_xe[e] + dot(xe[e], diag[e])
        side_s[e] = (-side * own_live[e + 1]).astype(BF16)
        following += dot(side_s[e], toward[e])
    part_b[...] = following.astype(BF16)

    @pl.when(jnp.logical_not(later[far]))
    def _():
        sums_b.start()

    @pl.when(later[far])
    def _():
        pl.semaphore_wait(hello.at[far], 1)
        for copy in first[far] + [sums_a, sums_b]:
            copy.start()


    arrival(toward, 0, far).wait_recv()
    square += dot(xe[far], toward[far])
    s0[...] = (three - square * own_live[0]).astype(BF16)
    for e in near:
        post(s0, s0_in, 2, e).start()
    added = dot(s0[...], x0)
    arrival(diag, 1, far).wait_recv()
    side = x0_xe[far] + dot(xe[far], diag[far])
    side_s[far] = (-side * own_live[far + 1]).astype(BF16)
    added += dot(side_s[far], toward[far])
    y0[...] = (0.5 * (following + added) * own_live[0]).astype(BF16)
    for e in near:
        post(y0, y0_in, 3, e).start()

    ye = []
    near_part = []
    for e in range(4):
        side = dot(s0[...], xe[e]) + dot(side_s[e], diag[e])
        ye.append((0.5 * side * own_live[e + 1]).astype(BF16))
        theirs = dot(toward[e], x0) + dot(diag[e], toward[e])
        theirs = (-theirs * near_live[e]).astype(BF16)
        near_part.append(dot(theirs, x0))
    far_square = dot(toward[far], xe[far])
    far_following = dot(theirs, xe[far])
    square = dot(y0[...], y0[...])
    y0_ye = [dot(y0[...], ye[e]) for e in range(4)]
    near_y = [None] * 4
    for e in near:
        arrival(s0_in, 2, e).wait_recv()
        theirs = near_part[e] + dot(s0_in[e], toward[e])
        near_y[e] = (0.5 * theirs * near_live[e]).astype(BF16)
        square += dot(ye[e], near_y[e])
    arrival(s0_in, 2, far).wait_recv()
    far_s0 = (three - (far_square + s0_in[far].astype(F32)) * far_live).astype(BF16)
    theirs = near_part[far] + dot(far_s0, toward[far])
    near_y[far] = (0.5 * theirs * near_live[far]).astype(BF16)
    square += dot(ye[far], near_y[far])
    last_s = (three - square * own_live[0]).astype(BF16)
    far_following += dot(far_s0, diag[far])
    results = [dot(last_s, y0[...])] + [dot(last_s, ye[e]) for e in range(4)]
    for e in range(4):
        arrival(y0_in, 3, e).wait_recv()
        theirs = y0_in[e]
        if e == far:
            theirs = (0.5 * (far_following + theirs.astype(F32)) * far_live).astype(BF16)
        side = y0_ye[e] + dot(ye[e], theirs)
        side = (-side * own_live[e + 1]).astype(BF16)
        results[0] += dot(side, near_y[e])
        results[e + 1] += dot(side, theirs)

    place_id = lax.broadcasted_iota(jnp.int32, (slots, 1), 0)
    holder = jnp.zeros((slots, 1), jnp.int32)
    for g in range(5):
        holder = jnp.where(place_id // 2 == g, devices[g], holder)
    candidate = (2 * holder + place_id % 2).astype(F32)
    for i in range(2):
        chosen = []
        for j in range(slots // 2):
            names = jnp.where(first_half, own[i][2 * j : 2 * j + 1], own[i][2 * j + 1 : 2 * j + 2])
            chosen.append(candidate == names)
        sums = [jnp.zeros((block, pair), F32) for _ in range(5)]
        for g in range(5):
            both = 0.5 * results[g][i * block : (i + 1) * block, :]
            turned = pltpu.roll(both, block, 1)
            for spot, doubled in (
                (2 * g, jnp.where(first_half, both, turned)),
                (2 * g + 1, jnp.where(first_half, turned, both)),
            ):
                for j in range(slots // 2):
                    sums[j] = jnp.where(chosen[j][spot : spot + 1], doubled, sums[j])
        for j in range(slots // 2):
            out[i, :, j * pair : (j + 1) * pair] = sums[j]
    for copy in sent:
        copy.wait_send()


def opening(out):
    out[...] = jnp.zeros_like(out)


def per_device(xvals, cols, counts):
    rows_here, block, _ = xvals.shape
    slots = cols.shape[1]
    row_count = lax.axis_size("row")
    col_count = lax.axis_size("col")
    width = rows_here * col_count
    pair = 2 * block
    square = (pair, pair)
    inside = pl.BlockSpec(memory_space=pltpu.VMEM)
    opened = pl.pallas_call(
        opening,
        out_shape=jax.ShapeDtypeStruct((8, 128), F32),
        compiler_params=pltpu.CompilerParams(vmem_limit_bytes=1024 * 1024),
        cost_estimate=pl.CostEstimate(flops=20000000000, bytes_accessed=20_000_000, transcendentals=0),
        name="opening",
    )()
    return pl.pallas_call(
        functools.partial(kernel, row_count, col_count, block, slots),
        out_shape=jax.ShapeDtypeStruct(xvals.shape, F32),
        in_specs=[inside] * 3 + [pl.BlockSpec(memory_space=pl.ANY)],
        out_specs=inside,
        scratch_shapes=[
            pltpu.VMEM((5,) + square, BF16),
            pltpu.VMEM((4,) + square, BF16),
            pltpu.VMEM((4,) + square, BF16),
            pltpu.VMEM(square, BF16),
            pltpu.VMEM((4,) + square, BF16),
            pltpu.VMEM(square, BF16),
            pltpu.VMEM((4,) + square, BF16),
            pltpu.VMEM(square, BF16),
            pltpu.VMEM(square, BF16),
            pltpu.SemaphoreType.DMA((4, 4)),
            pltpu.SemaphoreType.DMA((4, 4)),
            pltpu.SemaphoreType.REGULAR((4,)),
        ],
        compiler_params=pltpu.CompilerParams(
            collective_id=0, has_side_effects=True, vmem_limit_bytes=16 * 1024 * 1024
        ),
        cost_estimate=pl.CostEstimate(
            flops=250_000_000, bytes_accessed=600_000, transcendentals=0
        ),
        name="sign_steps",
    )(xvals, cols.T, counts.reshape(row_count, width), opened)


def solution(mesh):
    return jax.shard_map(
        per_device,
        mesh=mesh,
        in_specs=(P(("row", "col"), None, None), P(), P()),
        out_specs=P(("row", "col"), None, None),
        check_vma=False,
    )
```

```python
import functools

import jax
import jax.numpy as jnp
from jax import lax
from jax.experimental import pallas as pl
from jax.experimental.pallas import tpu as pltpu
from jax.sharding import PartitionSpec as P

MESH = pl.DeviceIdType.MESH
F32 = jnp.float32
BF16 = jnp.bfloat16


def dot(a, b):
    return jnp.dot(a, b, preferred_element_type=F32)


def kernel(
    row_count, col_count, block, slots,
    xs, all_cols, cnts, _, out,
    can, toward, diag, s0, s0_in, y0, y0_in, part_a, part_b,
    send_sem, recv_sem, hello,
):
    pair = 2 * block
    r = lax.axis_index("row")
    c = lax.axis_index("col")
    up, down = lax.rem(r + row_count - 1, row_count), lax.rem(r + 1, row_count)
    odd = lax.rem(c, 2)
    beside = c + 1 - 2 * odd
    beyond = lax.rem(c + col_count - 1 + 2 * odd, col_count)
    places = [(up, c), (down, c), (r, beside), (r, beyond)]
    back = (1, 0, 2, 3)
    near, far = (0, 1, 2), 3

    width = 2 * col_count
    tiles = [
        all_cols[:, pl.ds(pl.multiple_of(grid_row * width, width), width)]
        for grid_row in (r, up, down)
    ]

    def rank(row, col):
        z = lax.rem(lax.div(col, 2), 4) * 4 + lax.div(row, 4)
        usual = (z * 64 + lax.div(col, 8)) * 8 + lax.rem(row, 4) * 2 + lax.rem(col, 2)
        return jnp.where(row + col == 0, 12 * 512 - 1, usual)

    mine = rank(r, c)
    later = [rank(*place) > mine for place in places]
    barrier = pltpu.get_barrier_semaphore()
    for e in range(4):

        @pl.when(later[e])
        def _(e=e):
            pl.semaphore_signal(barrier, inc=1, device_id=places[e], device_id_type=MESH)

    lane = lax.broadcasted_iota(jnp.int32, (1, pair), 1)
    second = (lane >= block).astype(jnp.int32)
    tile_lane = lax.broadcasted_iota(jnp.int32, (1, width), 1)
    slot_id = lax.broadcasted_iota(jnp.int32, (slots, 1), 0).astype(F32)
    devices = [r * col_count + c] + [a * col_count + b for a, b in places]
    wide = [(2 * device + second).astype(F32) for device in devices]

    def stored_row(at, grid_row, grid_col, which):
        here = tile_lane == 2 * grid_col + which
        ids = jnp.sum(jnp.where(here, tiles[at].astype(F32), 0.0), axis=1, keepdims=True)
        count_row = cnts[pl.ds(grid_row, 1), :].astype(F32)
        count = jnp.sum(jnp.where(here, count_row, 0.0), axis=1, keepdims=True)
        return jnp.where(slot_id < count, ids, -1.0)

    own = [stored_row(0, r, c, which) for which in range(2)]
    masks = [[(own[i] == wide[g]) for g in range(5)] for i in range(2)]

    earlier = sum(1 - late.astype(jnp.int32) for late in later)

    @pl.when(earlier > 0)
    def _():
        pl.semaphore_wait(barrier, earlier)

    for e in range(4):

        @pl.when(jnp.logical_not(later[e]))
        def _(e=e):
            pl.semaphore_signal(
                hello.at[back[e]], inc=1, device_id=places[e], device_id_type=MESH
            )

    def live(parts):
        return jnp.concatenate(
            [
                jnp.broadcast_to(
                    jnp.max(part.astype(F32), axis=0, keepdims=True), (block, pair)
                )
                for part in parts
            ],
            axis=0,
        )

    first_half = lane < block
    sent = []

    def post(src, dst, kind, e):
        copy = pltpu.make_async_remote_copy(
            src_ref=src,
            dst_ref=dst.at[back[e]],
            send_sem=send_sem.at[kind, e],
            recv_sem=recv_sem.at[kind, back[e]],
            device_id=places[e],
            device_id_type=MESH,
        )
        sent.append(copy)
        return copy

    def arrival(dst, kind, e):
        return pltpu.make_async_remote_copy(
            src_ref=dst.at[e],
            dst_ref=dst.at[e],
            send_sem=send_sem.at[kind, e],
            recv_sem=recv_sem.at[kind, e],
            device_id=places[e],
            device_id_type=MESH,
        )

    first = [
        [post(can.at[e + 1], toward, 0, e), post(can.at[0], diag, 1, e)] for e in range(4)
    ]
    sums_a = post(part_a, s0_in, 2, far)
    sums_b = post(part_b, y0_in, 3, far)

    def arrange(groups):
        for i in range(2):
            sums = [jnp.zeros((block, pair), F32) for _ in groups]
            for j in range(slots // 2):
                both = xs[i, :, j * pair : (j + 1) * pair].astype(F32)
                turned = pltpu.roll(both, block, 1)
                for slot, doubled in (
                    (2 * j, jnp.where(first_half, both, turned)),
                    (2 * j + 1, jnp.where(first_half, turned, both)),
                ):
                    for k, g in enumerate(groups):
                        chosen = masks[i][g][slot : slot + 1]
                        sums[k] = jnp.where(chosen, doubled, sums[k])
            for k, g in enumerate(groups):
                can[g, i * block : (i + 1) * block, :] = sums[k].astype(BF16)

    arrange((far + 1, 0))

    @pl.when(jnp.logical_not(later[far]))
    def _():
        for copy in first[far]:
            copy.start()

    arrange((1, 2, 3))
    for e in near:

        @pl.when(jnp.logical_not(later[e]))
        def _(e=e):
            for copy in first[e]:
                copy.start()

    for e in near[::-1]:

        @pl.when(later[e])
        def _(e=e):
            pl.semaphore_wait(hello.at[e], 1)
            for copy in first[e]:
                copy.start()

    own_live = [live([masks[i][g] for i in range(2)]) for g in range(5)]
    near_live = []
    for e, (at, (grid_row, grid_col)) in enumerate(zip((1, 2, 0, 0), places)):
        rows = [stored_row(at, grid_row, grid_col, which) for which in range(2)]
        near_live.append(live([row == wide[0] for row in rows]))
        if e == far:
            far_live = live([row == wide[far + 1] for row in rows])
    x0 = can[0]
    xe = [can[e + 1] for e in range(4)]
    square = dot(x0, x0)
    x0_xe = [dot(x0, xe[e]) for e in range(4)]
    eye = lax.broadcasted_iota(jnp.int32, (pair, pair), 0) == lax.broadcasted_iota(
        jnp.int32, (pair, pair), 1
    )
    three = jnp.where(eye, 3.0, 0.0)

    for e in near:
        arrival(toward, 0, e).wait_recv()
        square += dot(xe[e], toward[e])
    part_a[...] = square.astype(BF16)

    @pl.when(jnp.logical_not(later[far]))
    def _():
        sums_a.start()

    side_s = [None] * 4
    following = jnp.zeros((pair, pair), F32)
    for e in near:
        arrival(diag, 1, e).wait_recv()
        side = x0_xe[e] + dot(xe[e], diag[e])
        side_s[e] = (-side * own_live[e + 1]).astype(BF16)
        following += dot(side_s[e], toward[e])
    part_b[...] = following.astype(BF16)

    @pl.when(jnp.logical_not(later[far]))
    def _():
        sums_b.start()

    arrival(toward, 0, far).wait_recv()
    square += dot(xe[far], toward[far])
    s0[...] = (three - square * own_live[0]).astype(BF16)
    for e in (1, 0, 2):
        post(s0, s0_in, 2, e).start()
    added = dot(s0[...], x0)
    arrival(diag, 1, far).wait_recv()
    side = x0_xe[far] + dot(xe[far], diag[far])
    side_s[far] = (-side * own_live[far + 1]).astype(BF16)
    added += dot(side_s[far], toward[far])
    y0[...] = (0.5 * (following + added) * own_live[0]).astype(BF16)
    for e in (1, 0, 2):
        post(y0, y0_in, 3, e).start()

    @pl.when(later[far])
    def _():
        pl.semaphore_wait(hello.at[far], 1)
        for copy in first[far] + [sums_a, sums_b]:
            copy.start()


    ye = []
    near_part = []
    for e in range(4):
        side = dot(s0[...], xe[e]) + dot(side_s[e], diag[e])
        ye.append((0.5 * side * own_live[e + 1]).astype(BF16))
        theirs = dot(toward[e], x0) + dot(diag[e], toward[e])
        theirs = (-theirs * near_live[e]).astype(BF16)
        near_part.append(dot(theirs, x0))
    far_square = dot(toward[far], xe[far])
    far_following = dot(theirs, xe[far])
    square = dot(y0[...], y0[...])
    y0_ye = [dot(y0[...], ye[e]) for e in range(4)]
    near_y = [None] * 4
    for e in (1, 2):
        arrival(s0_in, 2, e).wait_recv()
        theirs = near_part[e] + dot(s0_in[e], toward[e])
        near_y[e] = (0.5 * theirs * near_live[e]).astype(BF16)
        square += dot(ye[e], near_y[e])
    arrival(s0_in, 2, far).wait_recv()
    far_s0 = (three - (far_square + s0_in[far].astype(F32)) * far_live).astype(BF16)
    theirs = near_part[far] + dot(far_s0, toward[far])
    near_y[far] = (0.5 * theirs * near_live[far]).astype(BF16)
    square += dot(ye[far], near_y[far])
    far_following += dot(far_s0, diag[far])
    for e in (0,):
        arrival(s0_in, 2, e).wait_recv()
        theirs = near_part[e] + dot(s0_in[e], toward[e])
        near_y[e] = (0.5 * theirs * near_live[e]).astype(BF16)
        square += dot(ye[e], near_y[e])
    last_s = (three - square * own_live[0]).astype(BF16)
    results = [dot(last_s, y0[...])] + [dot(last_s, ye[e]) for e in range(4)]
    for e in (1, 2, 3, 0):
        arrival(y0_in, 3, e).wait_recv()
        theirs = y0_in[e]
        if e == far:
            theirs = (0.5 * (far_following + theirs.astype(F32)) * far_live).astype(BF16)
        side = y0_ye[e] + dot(ye[e], theirs)
        side = (-side * own_live[e + 1]).astype(BF16)
        results[0] += dot(side, near_y[e])
        results[e + 1] += dot(side, theirs)

    place_id = lax.broadcasted_iota(jnp.int32, (slots, 1), 0)
    holder = jnp.zeros((slots, 1), jnp.int32)
    for g in range(5):
        holder = jnp.where(place_id // 2 == g, devices[g], holder)
    candidate = (2 * holder + place_id % 2).astype(F32)
    for i in range(2):
        chosen = []
        for j in range(slots // 2):
            names = jnp.where(first_half, own[i][2 * j : 2 * j + 1], own[i][2 * j + 1 : 2 * j + 2])
            chosen.append(candidate == names)
        sums = [jnp.zeros((block, pair), F32) for _ in range(5)]
        for g in range(5):
            both = 0.5 * results[g][i * block : (i + 1) * block, :]
            turned = pltpu.roll(both, block, 1)
            for spot, doubled in (
                (2 * g, jnp.where(first_half, both, turned)),
                (2 * g + 1, jnp.where(first_half, turned, both)),
            ):
                for j in range(slots // 2):
                    sums[j] = jnp.where(chosen[j][spot : spot + 1], doubled, sums[j])
        for j in range(slots // 2):
            out[i, :, j * pair : (j + 1) * pair] = sums[j]
    for copy in sent:
        copy.wait_send()


def opening(out):
    out[...] = jnp.zeros_like(out)


def per_device(xvals, cols, counts):
    rows_here, block, _ = xvals.shape
    slots = cols.shape[1]
    row_count = lax.axis_size("row")
    col_count = lax.axis_size("col")
    width = rows_here * col_count
    pair = 2 * block
    square = (pair, pair)
    inside = pl.BlockSpec(memory_space=pltpu.VMEM)
    opened = pl.pallas_call(
        opening,
        out_shape=jax.ShapeDtypeStruct((8, 128), F32),
        compiler_params=pltpu.CompilerParams(vmem_limit_bytes=1024 * 1024),
        cost_estimate=pl.CostEstimate(flops=20000000000, bytes_accessed=20_000_000, transcendentals=0),
        name="opening",
    )()
    return pl.pallas_call(
        functools.partial(kernel, row_count, col_count, block, slots),
        out_shape=jax.ShapeDtypeStruct(xvals.shape, F32),
        in_specs=[inside] * 3 + [pl.BlockSpec(memory_space=pl.ANY)],
        out_specs=inside,
        scratch_shapes=[
            pltpu.VMEM((5,) + square, BF16),
            pltpu.VMEM((4,) + square, BF16),
            pltpu.VMEM((4,) + square, BF16),
            pltpu.VMEM(square, BF16),
            pltpu.VMEM((4,) + square, BF16),
            pltpu.VMEM(square, BF16),
            pltpu.VMEM((4,) + square, BF16),
            pltpu.VMEM(square, BF16),
            pltpu.VMEM(square, BF16),
            pltpu.SemaphoreType.DMA((4, 4)),
            pltpu.SemaphoreType.DMA((4, 4)),
            pltpu.SemaphoreType.REGULAR((4,)),
        ],
        compiler_params=pltpu.CompilerParams(
            collective_id=0, has_side_effects=True, vmem_limit_bytes=16 * 1024 * 1024
        ),
        cost_estimate=pl.CostEstimate(
            flops=250_000_000, bytes_accessed=600_000, transcendentals=0
        ),
        name="sign_steps",
    )(xvals, cols.T, counts.reshape(row_count, width), opened)


def solution(mesh):
    return jax.shard_map(
        per_device,
        mesh=mesh,
        in_specs=(P(("row", "col"), None, None), P(), P()),
        out_specs=P(("row", "col"), None, None),
        check_vma=False,
    )
```
